256 devices in a mesh: wide: 32 (over x, z_hi, core), tp: 8 (over z_lo, y).
Axes of the slice: x: 4, y: 4, z: 8 (z_hi: 4, z_lo: 2; z = z_hi * 2 + z_lo), core: 2. Of those that a mesh axis runs over, the one named last changes fastest.
Arguments:
- master_weight: float32 [14848, 4096], P('tp', 'wide'), may hold values from -0.046875 to 0.046875
- first_moment: float32 [14848, 4096], P('tp', 'wide'), may hold values from -0.06 to 0.06
- second_moment: float32 [14848, 4096], P('tp', 'wide'), may hold values from 1e-06 to 0.0001
- gradient: float32 [14848, 4096], P('tp', 'wide'), may hold values from -0.06 to 0.06
- gate_preact: bfloat16 [16384, 14848], P('wide', 'tp'), may hold values from -6 to 6
- up_preact: bfloat16 [16384, 14848], P('wide', 'tp'), may hold values from -6 to 6
Outputs:
- new_weight: float32 [14848, 4096], P('tp', 'wide')
- new_first: float32 [14848, 4096], P('tp', 'wide')
- new_second: float32 [14848, 4096], P('tp', 'wide')
- ffn_output: bfloat16 [16384, 4096], P('wide', 'tp')
The draws below stay inside these ranges and needn't reach their ends.
All inputs are finite; a program needn't handle non-finite values.
Results may differ from the reference program's by a relative error of at most 0.0057.
Values may be sent and summed in bfloat16 or wider, within the bound.
No kernel may reach another device: no remote copies, remote signals or barrier semaphores. Data moves between devices by JAX's collectives and lax.ppermute only.
A program may use at most 128 MiB of HBM per device.

```python
import math
import jax
import jax.numpy as jnp
from jax import lax

D = 4096
FF = 14848
TOK_DEV = 512
TOKENS = 16384
N_WIDE = 32


def block_scale(own_key, dims, cuts, smallest, largest):
    loudness = 1.0
    for axis_at, parts in cuts:
        heights = jax.random.uniform(jax.random.fold_in(jax.random.fold_in(own_key, 6), axis_at), (parts,), jnp.float32, smallest / len(cuts), largest / len(cuts))
        loudness = loudness * jnp.repeat(jnp.exp(heights), dims[axis_at] // parts).reshape((-1,) + (1,) * (len(dims) - 1 - axis_at))
    return loudness


def scatter_about(own_key, dims, spread, reach, shards=(), held_as=jnp.bfloat16):
    array = spread * jax.random.normal(own_key, dims, jnp.float32)
    if shards:
        array = array * block_scale(own_key, dims, shards, -0.22, 0.18)
    return jnp.clip(array, -reach, reach).astype(held_as)


def setup_inputs(seed: int = 0) -> dict:
    seeds = jax.random.split(jax.random.key(seed), 7)
    master_weight = scatter_about(seeds[0], (FF, D), FF ** -0.5, 0.046875, ((0, 8), (1, 32)), jnp.float32)
    first_moment = scatter_about(seeds[1], (FF, D), 0.01, 0.06, ((0, 8), (1, 32)), jnp.float32)
    second_moment = jnp.clip(jnp.exp(math.log(0.0001) - 4.6051702 * jax.random.uniform(seeds[2], (FF, D), jnp.float32) ** block_scale(seeds[2], (FF, D), ((0, 8), (1, 32)), -0.2, 0.2)), 9.999999974752427e-07, 0.0001)
    gradient = scatter_about(seeds[3], (FF, D), 0.01, 0.06, ((0, 8), (1, 32)), jnp.float32)
    gate_preact = scatter_about(seeds[4], (TOKENS, FF), 1.0, 6.0, ((0, 32), (1, 8)))
    up_preact = scatter_about(seeds[5], (TOKENS, FF), 1.0, 6.0, ((0, 32), (1, 8)))
    return dict(master_weight=master_weight, first_moment=first_moment, second_moment=second_moment, gradient=gradient, gate_preact=gate_preact, up_preact=up_preact)


beta_one = 0.9
beta_two = 0.95
learn_rate = 0.003
decay_rate = 0.1
epsilon = 1e-08

def reference(master_weight, first_moment, second_moment, gradient, gate_preact, up_preact):
    new_first = beta_one * first_moment + (1.0 - beta_one) * gradient
    new_second = beta_two * second_moment + (1.0 - beta_two) * gradient * gradient
    corr_one = 1.0 - beta_one ** 10
    corr_two = 1.0 - beta_two ** 10
    update = new_first / corr_one / (jnp.sqrt(new_second / corr_two) + epsilon)
    new_weight = master_weight - learn_rate * (update + decay_rate * master_weight)
    rollout_weight = new_weight.astype(jnp.bfloat16)
    gate_blocks = gate_preact.reshape(N_WIDE, TOK_DEV, FF)
    up_blocks = up_preact.reshape(N_WIDE, TOK_DEV, FF)

    def one_block(pair):
        gate_rows, up_rows = pair
        hidden = (jax.nn.silu(gate_rows.astype(jnp.float32)) * up_rows.astype(jnp.float32)).astype(jnp.bfloat16)
        return jnp.dot(hidden, rollout_weight, preferred_element_type=jnp.float32).astype(jnp.bfloat16)
    ffn_output = lax.map(one_block, (gate_blocks, up_blocks)).reshape(TOKENS, D)
    return (new_weight, new_first, new_second, ffn_output)
```

```python
import jax
import jax.numpy as jnp
from jax import lax
from jax.sharding import Mesh
from jax.sharding import PartitionSpec as P

beta_one = 0.9
beta_two = 0.95
learn_rate = 0.003
decay_rate = 0.1
epsilon = 1e-08

X, ZH, C, ZL, Y = 4, 4, 2, 2, 4
f32 = jnp.float32
bf16 = jnp.bfloat16


def shift(n, k):
    return [(i, (i + k) % n) for i in range(n)]


def by_core(n):
    return [(2 * i + c, 2 * ((i + (1 - 2 * c)) % n) + c) for i in range(n) for c in range(2)]


def adamw(master_weight, first_moment, second_moment, gradient):
    new_first = beta_one * first_moment + (1.0 - beta_one) * gradient
    new_second = beta_two * second_moment + (1.0 - beta_two) * gradient * gradient
    corr_one = 1.0 - beta_one**10
    corr_two = 1.0 - beta_two**10
    update = new_first / corr_one / (jnp.sqrt(new_second / corr_two) + epsilon)
    new_weight = master_weight - learn_rate * (update + decay_rate * master_weight)
    return new_weight, new_first, new_second


def body(master_weight, first_moment, second_moment, gradient, gate_preact, up_preact):
    x, zh, c, zl, y = (lax.axis_index(a) for a in ("x", "zh", "c", "zl", "y"))
    new_weight, new_first, new_second = adamw(master_weight, first_moment, second_moment, gradient)
    own = new_weight.astype(bf16)

    def go(v, axis, k):
        return lax.ppermute(v, axis, shift({"x": X, "zh": ZH, "y": Y}[axis], k))

    def go_by_core(low, high, axis):
        return lax.ppermute(jnp.where(c == 0, low, high), (axis, "c"), by_core(4))

    blk = {(0, 0): own}
    blk[0, 3] = go(own, "zh", 1)
    blk[0, 1] = go(own, "zh", -1)
    blk[3, 0] = go(own, "x", 1)
    blk[1, 0] = go(own, "x", -1)

    hidden = (jax.nn.silu(gate_preact.astype(f32)) * up_preact.astype(f32)).astype(bf16)
    other = lax.ppermute(hidden, "c", shift(C, 1))
    both = jnp.concatenate([hidden, other], axis=0)

    blk[0, 2] = go_by_core(blk[0, 3], blk[0, 1], "zh")
    blk[2, 0] = go_by_core(blk[3, 0], blk[1, 0], "x")
    for k in (3, 1, 2):
        blk[3, k] = go(blk[0, k], "x", 1)
        blk[1, k] = go(blk[0, k], "x", -1)
    blk[2, 3] = go(blk[3, 3], "x", 1)
    blk[2, 1] = go(blk[1, 1], "x", -1)
    blk[2, 2] = go_by_core(blk[3, 2], blk[1, 2], "x")

    def summed(xs, ks):
        parts, homes = [], []
        for dx in xs:
            for k in ks:
                parts.append(jnp.dot(both, blk[dx, k], preferred_element_type=f32).astype(bf16))
                homes.append(2 * ((x + dx) % 2) + ((zh + k) % 4) // 2)

        def meant_for(d):
            at = (y + d) % Y
            v = parts[3]
            for p, h in zip(parts[:3], homes[:3]):
                v = jnp.where(h == at, p, v)
            return v

        total = meant_for(0).astype(f32)
        for d in (1, 3, 2):
            total = total + go(meant_for(d), "y", d).astype(f32)
        return total.astype(bf16)

    def finished(near, far):
        near_x = jnp.where(x % 2 == y // 2, x, (x + 3) % X)
        keep_near = near_x // 2 == zl
        keep = jnp.where(keep_near, near, far)
        send = jnp.where(keep_near, far, near)
        value = (keep.astype(f32) + lax.ppermute(send, "zl", shift(ZL, 1)).astype(f32)).astype(bf16)
        return value[:512], lax.ppermute(value[512:], "c", shift(C, 1))

    near_odd = summed((0, 3), (1, 3))
    near_even = summed((0, 3), (0, 2))
    far_odd = summed((2, 1), (1, 3))
    odd = finished(near_odd, far_odd)
    far_even = summed((2, 1), (0, 2))
    even = finished(near_even, far_even)

    columns = []
    for a in range(2):
        for b in range(2):
            mine = jnp.where(zh % 2 == a, even[0], odd[0])
            theirs = jnp.where(zh % 2 == a, even[1], odd[1])
            columns.append(jnp.where(c == b, mine, theirs))
    return (new_weight, new_first, new_second, jnp.concatenate(columns, axis=1))


def solution(mesh):
    fine = Mesh(mesh.devices.reshape(X, ZH, C, ZL, Y), ("x", "zh", "c", "zl", "y"))
    wide, tp = ("x", "zh", "c"), ("zl", "y")
    in_specs = (P(tp, wide),) * 4 + (P(wide, tp),) * 2
    out_specs = (P(tp, wide),) * 3 + (P(wide, tp),)
    return jax.shard_map(body, mesh=fine, in_specs=in_specs, out_specs=out_specs, check_vma=False)
```

```python
import jax
import jax.numpy as jnp
from jax import lax
from jax.experimental import pallas as pl
from jax.experimental.pallas import tpu as pltpu
from jax.sharding import Mesh
from jax.sharding import PartitionSpec as P

beta_one = 0.9
beta_two = 0.95
learn_rate = 0.003
decay_rate = 0.1
epsilon = 1e-08

X, ZH, C, ZL, Y = 4, 4, 2, 2, 4
SIZES = {"x": X, "zh": ZH, "c": C, "zl": ZL, "y": Y}
f32 = jnp.float32
bf16 = jnp.bfloat16
SLOW = pl.CostEstimate(flops=10**10, bytes_accessed=40 * 2**20, transcendentals=0)


def adamw(master_weight, first_moment, second_moment, gradient):
    new_first = beta_one * first_moment + (1.0 - beta_one) * gradient
    new_second = beta_two * second_moment + (1.0 - beta_two) * gradient * gradient
    corr_one = 1.0 - beta_one**10
    corr_two = 1.0 - beta_two**10
    update = new_first / corr_one / (jnp.sqrt(new_second / corr_two) + epsilon)
    new_weight = master_weight - learn_rate * (update + decay_rate * master_weight)
    return new_weight, new_first, new_second


def shift(v, axis, k):
    n = SIZES[axis]
    return lax.ppermute(v, axis, [(i, (i + k) % n) for i in range(n)])


def flip(v, axis, k):
    return lax.ppermute(v, axis, [(i, i ^ k) for i in range(SIZES[axis])])


def in_order(*values):
    return lax.optimization_barrier(values)


def hidden_kernel(gate_ref, up_ref, out_ref):
    gate = gate_ref[...].astype(f32)
    value = gate / (1.0 + jnp.exp(-gate)) * up_ref[...].astype(f32)
    depth = value.shape[0]
    out_ref[:, :depth] = value.astype(bf16).T
    out_ref[:, depth:] = jnp.zeros((128, out_ref.shape[1] - depth), bf16)


def hidden_of(gate, up):
    depth, tokens = gate.shape
    wide = -(-depth // 128) * 128
    block = pl.BlockSpec((depth, 128), lambda i: (0, i))
    return pl.pallas_call(
        hidden_kernel,
        grid=(tokens // 128,),
        out_shape=jax.ShapeDtypeStruct((tokens, wide), bf16),
        in_specs=[block, block],
        out_specs=pl.BlockSpec((128, wide), lambda i: (i, 0)),
        compiler_params=pltpu.CompilerParams(vmem_limit_bytes=16 * 2**20),
        cost_estimate=SLOW,
    )(gate, up)


def round_kernel(q_ref, mine_ref, other_ref, *refs):
    blocks, outs = refs[:4], refs[4:]

    for q in range(4):

        @pl.when(q_ref[0] == q)
        def _():
            for part, rows_ref in enumerate((mine_ref, other_ref)):
                rows = rows_ref[:, : blocks[0].shape[0]]
                for m in (0, 2):
                    pair = jnp.concatenate([blocks[m][...], blocks[m + 1][...]], axis=1)
                    value = jnp.dot(rows, pair, preferred_element_type=f32).astype(bf16)
                    for j in range(2):
                        place = pl.ds(part * 512, 512)
                        outs[(m + j) ^ q][place] = value[:, j * 128 : (j + 1) * 128]


def round_of(q, mine, other, blocks):
    return pl.pallas_call(
        round_kernel,
        out_shape=[jax.ShapeDtypeStruct((1024, 128), bf16)] * 4,
        in_specs=[pl.BlockSpec(memory_space=pltpu.SMEM)] + [pl.BlockSpec(memory_space=pltpu.VMEM)] * 6,
        out_specs=[pl.BlockSpec(memory_space=pltpu.VMEM)] * 4,
        compiler_params=pltpu.CompilerParams(vmem_limit_bytes=24 * 2**20),
        cost_estimate=SLOW,
    )(q, mine, other, *blocks)


def body(master_weight, first_moment, second_moment, gradient, gate_preact, up_preact):
    x, zh, c, zl, y = (lax.axis_index(a) for a in ("x", "zh", "c", "zl", "y"))
    new_weight, new_first, new_second = adamw(master_weight, first_moment, second_moment, gradient)
    own = new_weight.astype(bf16)

    def by_core(low, high, axis, move):
        pairs = [(2 * i + k, 2 * move(i, k) + k) for i in range(4) for k in range(2)]
        return lax.ppermute(jnp.where(c == 0, low, high), (axis, "c"), pairs)

    def onward(b3, b1):
        return by_core(b3, b1, "x", lambda i, k: (i + 1 - 2 * k) % X)

    q = (((x & 1) << 1) | (zh >> 1)) ^ y
    q = jnp.full((1,), q, jnp.int32)

    x20 = shift(own, "x", 2)
    x10 = shift(own, "x", -1)
    x30 = shift(own, "x", 1)
    z1 = flip(own, "zh", 1)
    z3 = flip(own, "zh", 3)
    gate_preact, up_preact, own = in_order(gate_preact, up_preact, own)
    hidden = hidden_of(gate_preact.T, up_preact.T)
    x20, x10, x30, z1, z3, hidden = in_order(x20, x10, x30, z1, z3, hidden)

    other = shift(hidden, "c", 1)
    z2 = by_core(z3, z1, "zh", lambda i, k: i ^ (1 if k == 0 else 3))
    x33 = shift(z3, "x", 1)
    x13 = shift(z3, "x", -1)
    x33, x13, z2, z1, other = in_order(x33, x13, z2, z1, other)

    def sent(parts):
        return [parts[0]] + [flip(parts[d], "y", d) for d in (1, 3, 2)]

    def summed(parts):
        total = parts[0].astype(f32)
        for part in parts[1:]:
            total = total + part.astype(f32)
        return total.astype(bf16)

    x23 = onward(x33, x13)
    x31 = shift(z1, "x", 1)
    x11 = shift(z1, "x", -1)
    near_a = sent(round_of(q, hidden, other, [own, z3, x30, x33]))
    x23, z2 = in_order(x23, z2)
    far_a = sent(round_of(q, hidden, other, [x20, x23, x10, x13]))
    x31, x11, z2 = in_order(x31, x11, z2)

    x32 = shift(z2, "x", 1)
    x12 = shift(z2, "x", -1)
    x21 = onward(x31, x11)
    x32, x12, *near_a = in_order(x32, x12, *near_a)
    near_a = summed(near_a)

    x22 = onward(x32, x12)
    near_b = sent(round_of(q, hidden, other, [z1, z2, x31, x32]))
    x21, x22, *far_a = in_order(x21, x22, *far_a)
    far_a = summed(far_a)

    def finished(near, far):
        near_x = jnp.where((x & 1) == (y >> 1), x, (x + 3) & 3)
        keep_near = (near_x >> 1) == zl
        keep = jnp.where(keep_near, near, far)
        send = jnp.where(keep_near, far, near)
        value = (keep.astype(f32) + flip(send, "zl", 1).astype(f32)).astype(bf16)
        return value[:512], flip(value[512:], "c", 1)

    first = finished(near_a, far_a)
    far_b = summed(sent(round_of(q, hidden, other, [x21, x22, x11, x12])))
    near_b = summed(near_b)
    second = finished(near_b, far_b)

    first_half = (zh & 1) ^ (zh >> 1) ^ (y & 1)
    columns = []
    for a in range(2):
        for b in range(2):
            mine = jnp.where(first_half == a, first[0], second[0])
            theirs = jnp.where(first_half == a, first[1], second[1])
            columns.append(jnp.where(c == b, mine, theirs))
    return (new_weight, new_first, new_second, jnp.concatenate(columns, axis=1))


def solution(mesh):
    fine = Mesh(mesh.devices.reshape(X, ZH, C, ZL, Y), ("x", "zh", "c", "zl", "y"))
    wide, tp = ("x", "zh", "c"), ("zl", "y")
    in_specs = (P(tp, wide),) * 4 + (P(wide, tp),) * 2
    out_specs = (P(tp, wide),) * 3 + (P(wide, tp),)
    return jax.shard_map(body, mesh=fine, in_specs=in_specs, out_specs=out_specs, check_vma=False)
```

```python
import jax
import jax.numpy as jnp
from jax import lax
from jax.experimental import pallas as pl
from jax.experimental.pallas import tpu as pltpu
from jax.sharding import Mesh
from jax.sharding import PartitionSpec as P

beta_one = 0.9
beta_two = 0.95
learn_rate = 0.003
decay_rate = 0.1
epsilon = 1e-08

X, ZH, C, ZL, Y = 4, 4, 2, 2, 4
SIZES = {"x": X, "zh": ZH, "c": C, "zl": ZL, "y": Y}
f32 = jnp.float32
bf16 = jnp.bfloat16
SLOW = pl.CostEstimate(flops=10**10, bytes_accessed=40 * 2**20, transcendentals=0)


def adamw(master_weight, first_moment, second_moment, gradient):
    new_first = beta_one * first_moment + (1.0 - beta_one) * gradient
    new_second = beta_two * second_moment + (1.0 - beta_two) * gradient * gradient
    corr_one = 1.0 - beta_one**10
    corr_two = 1.0 - beta_two**10
    update = new_first / corr_one / (jnp.sqrt(new_second / corr_two) + epsilon)
    new_weight = master_weight - learn_rate * (update + decay_rate * master_weight)
    return new_weight, new_first, new_second


def shift(v, axis, k):
    n = SIZES[axis]
    return lax.ppermute(v, axis, [(i, (i + k) % n) for i in range(n)])


def flip(v, axis, k):
    return lax.ppermute(v, axis, [(i, i ^ k) for i in range(SIZES[axis])])


def in_order(*values):
    return lax.optimization_barrier(values)


def hidden_kernel(gate_ref, up_ref, out_ref):
    gate = gate_ref[...].astype(f32)
    value = gate / (1.0 + jnp.exp(-gate)) * up_ref[...].astype(f32)
    depth = value.shape[0]
    out_ref[:, :depth] = value.astype(bf16).T
    out_ref[:, depth:] = jnp.zeros((128, out_ref.shape[1] - depth), bf16)


def hidden_of(gate, up):
    depth, tokens = gate.shape
    wide = -(-depth // 128) * 128
    block = pl.BlockSpec((depth, 128), lambda i: (0, i))
    return pl.pallas_call(
        hidden_kernel,
        grid=(tokens // 128,),
        out_shape=jax.ShapeDtypeStruct((tokens, wide), bf16),
        in_specs=[block, block],
        out_specs=pl.BlockSpec((128, wide), lambda i: (i, 0)),
        compiler_params=pltpu.CompilerParams(vmem_limit_bytes=16 * 2**20),
        cost_estimate=SLOW,
    )(gate, up)


def round_kernel(q_ref, mine_ref, other_ref, *refs):
    blocks, outs = refs[:4], refs[4:]

    for q in range(4):

        @pl.when(q_ref[0] == q)
        def _():
            for part, rows_ref in enumerate((mine_ref, other_ref)):
                rows = rows_ref[:, : blocks[0].shape[0]]
                for m in (0, 2):
                    pair = jnp.concatenate([blocks[m][...], blocks[m + 1][...]], axis=1)
                    value = jnp.dot(rows, pair, preferred_element_type=f32).astype(bf16)
                    for j in range(2):
                        place = pl.ds(part * 512, 512)
                        outs[(m + j) ^ q][place] = value[:, j * 128 : (j + 1) * 128]


def round_of(q, mine, other, blocks):
    return pl.pallas_call(
        round_kernel,
        out_shape=[jax.ShapeDtypeStruct((1024, 128), bf16)] * 4,
        in_specs=[pl.BlockSpec(memory_space=pltpu.SMEM)] + [pl.BlockSpec(memory_space=pltpu.VMEM)] * 6,
        out_specs=[pl.BlockSpec(memory_space=pltpu.VMEM)] * 4,
        compiler_params=pltpu.CompilerParams(vmem_limit_bytes=24 * 2**20),
        cost_estimate=SLOW,
    )(q, mine, other, *blocks)


def body(master_weight, first_moment, second_moment, gradient, gate_preact, up_preact):
    x, zh, c, zl, y = (lax.axis_index(a) for a in ("x", "zh", "c", "zl", "y"))
    states = (master_weight, first_moment, second_moment, gradient)
    own = adamw(*states)[0].astype(bf16)

    def by_core(low, high, axis, move):
        pairs = [(2 * i + k, 2 * move(i, k) + k) for i in range(4) for k in range(2)]
        return lax.ppermute(jnp.where(c == 0, low, high), (axis, "c"), pairs)

    def onward(b3, b1):
        return by_core(b3, b1, "x", lambda i, k: (i + 1 - 2 * k) % X)

    q = (((x & 1) << 1) | (zh >> 1)) ^ y
    q = jnp.full((1,), q, jnp.int32)

    x20 = shift(own, "x", 2)
    x10 = shift(own, "x", -1)
    x30 = shift(own, "x", 1)
    z1 = flip(own, "zh", 1)
    z3 = flip(own, "zh", 3)
    gate_preact, up_preact, own, *states = in_order(gate_preact, up_preact, own, *states)
    hidden = hidden_of(gate_preact.T, up_preact.T)
    news = adamw(*states)
    x20, x10, x30, z1, z3, hidden, *news = in_order(x20, x10, x30, z1, z3, hidden, *news)
    new_weight, new_first, new_second = news

    other = shift(hidden, "c", 1)
    z2 = by_core(z3, z1, "zh", lambda i, k: i ^ (1 if k == 0 else 3))
    x33 = shift(z3, "x", 1)
    x13 = shift(z3, "x", -1)
    x33, x13, z1, other = in_order(x33, x13, z1, other)

    def sent(parts):
        return [parts[0]] + [flip(parts[d], "y", d) for d in (1, 3, 2)]

    def summed(parts):
        total = parts[0].astype(f32)
        for part in parts[1:]:
            total = total + part.astype(f32)
        return total.astype(bf16)

    x23 = onward(x33, x13)
    x31 = shift(z1, "x", 1)
    x11 = shift(z1, "x", -1)
    near_a = sent(round_of(q, hidden, other, [own, z3, x30, x33]))
    x31, x11, z2 = in_order(x31, x11, z2)

    x32 = shift(z2, "x", 1)
    x12 = shift(z2, "x", -1)
    far_a = sent(round_of(q, hidden, other, [x20, x23, x10, x13]))
    x21 = onward(x31, x11)
    x32, x12, *near_a = in_order(x32, x12, *near_a)
    near_a = summed(near_a)

    x22 = onward(x32, x12)
    near_b = sent(round_of(q, hidden, other, [z1, z2, x31, x32]))
    x21, x22, *far_a = in_order(x21, x22, *far_a)
    far_a = summed(far_a)

    def finished(near, far):
        near_x = jnp.where((x & 1) == (y >> 1), x, (x + 3) & 3)
        keep_near = (near_x >> 1) == zl
        keep = jnp.where(keep_near, near, far)
        send = jnp.where(keep_near, far, near)
        value = (keep.astype(f32) + flip(send, "zl", 1).astype(f32)).astype(bf16)
        return value[:512], flip(value[512:], "c", 1)

    first = finished(near_a, far_a)
    far_b = summed(sent(round_of(q, hidden, other, [x21, x22, x11, x12])))
    near_b = summed(near_b)
    second = finished(near_b, far_b)

    first_half = (zh & 1) ^ (zh >> 1) ^ (y & 1)
    columns = []
    for a in range(2):
        for b in range(2):
            mine = jnp.where(first_half == a, first[0], second[0])
            theirs = jnp.where(first_half == a, first[1], second[1])
            columns.append(jnp.where(c == b, mine, theirs))
    return (new_weight, new_first, new_second, jnp.concatenate(columns, axis=1))


def solution(mesh):
    fine = Mesh(mesh.devices.reshape(X, ZH, C, ZL, Y), ("x", "zh", "c", "zl", "y"))
    wide, tp = ("x", "zh", "c"), ("zl", "y")
    in_specs = (P(tp, wide),) * 4 + (P(wide, tp),) * 2
    out_specs = (P(tp, wide),) * 3 + (P(wide, tp),)
    return jax.shard_map(body, mesh=fine, in_specs=in_specs, out_specs=out_specs, check_vma=False)
```

```python
import jax
import jax.numpy as jnp
from jax import lax
from jax.experimental import pallas as pl
from jax.experimental.pallas import tpu as pltpu
from jax.sharding import Mesh
from jax.sharding import PartitionSpec as P

beta_one = 0.9
beta_two = 0.95
learn_rate = 0.003
decay_rate = 0.1
epsilon = 1e-08

X, ZH, C, ZL, Y = 4, 4, 2, 2, 4
SIZES = {"x": X, "zh": ZH, "c": C, "zl": ZL, "y": Y}
f32 = jnp.float32
bf16 = jnp.bfloat16
SLOW = pl.CostEstimate(flops=10**10, bytes_accessed=40 * 2**20, transcendentals=0)


def adamw(master_weight, first_moment, second_moment, gradient):
    new_first = beta_one * first_moment + (1.0 - beta_one) * gradient
    new_second = beta_two * second_moment + (1.0 - beta_two) * gradient * gradient
    corr_one = 1.0 - beta_one**10
    corr_two = 1.0 - beta_two**10
    update = new_first / corr_one / (jnp.sqrt(new_second / corr_two) + epsilon)
    new_weight = master_weight - learn_rate * (update + decay_rate * master_weight)
    return new_weight, new_first, new_second


def shift(v, axis, k):
    n = SIZES[axis]
    return lax.ppermute(v, axis, [(i, (i + k) % n) for i in range(n)])


def flip(v, axis, k):
    return lax.ppermute(v, axis, [(i, i ^ k) for i in range(SIZES[axis])])


def in_order(*values):
    return lax.optimization_barrier(values)


def hidden_kernel(gate_ref, up_ref, out_ref):
    gate = gate_ref[...].astype(f32)
    value = gate / (1.0 + jnp.exp(-gate)) * up_ref[...].astype(f32)
    depth = value.shape[0]
    out_ref[:, :depth] = value.astype(bf16).T
    out_ref[:, depth:] = jnp.zeros((128, out_ref.shape[1] - depth), bf16)


def hidden_of(gate, up):
    depth, tokens = gate.shape
    wide = -(-depth // 128) * 128
    block = pl.BlockSpec((depth, 128), lambda i: (0, i))
    return pl.pallas_call(
        hidden_kernel,
        grid=(tokens // 128,),
        out_shape=jax.ShapeDtypeStruct((tokens, wide), bf16),
        in_specs=[block, block],
        out_specs=pl.BlockSpec((128, wide), lambda i: (i, 0)),
        compiler_params=pltpu.CompilerParams(vmem_limit_bytes=16 * 2**20),
        cost_estimate=SLOW,
    )(gate, up)


def round_kernel(q_ref, mine_ref, other_ref, *refs):
    blocks, outs = refs[:4], refs[4:]

    for q in range(4):

        @pl.when(q_ref[0] == q)
        def _():
            for part, rows_ref in enumerate((mine_ref, other_ref)):
                rows = rows_ref[:, : blocks[0].shape[0]]
                for m in (0, 2):
                    pair = jnp.concatenate([blocks[m][...], blocks[m + 1][...]], axis=1)
                    value = jnp.dot(rows, pair, preferred_element_type=f32).astype(bf16)
                    for j in range(2):
                        place = pl.ds(part * 512, 512)
                        outs[(m + j) ^ q][place] = value[:, j * 128 : (j + 1) * 128]


def round_of(q, mine, other, blocks):
    return pl.pallas_call(
        round_kernel,
        out_shape=[jax.ShapeDtypeStruct((1024, 128), bf16)] * 4,
        in_specs=[pl.BlockSpec(memory_space=pltpu.SMEM)] + [pl.BlockSpec(memory_space=pltpu.VMEM)] * 6,
        out_specs=[pl.BlockSpec(memory_space=pltpu.VMEM)] * 4,
        compiler_params=pltpu.CompilerParams(vmem_limit_bytes=24 * 2**20),
        cost_estimate=SLOW,
    )(q, mine, other, *blocks)


def body(master_weight, first_moment, second_moment, gradient, gate_preact, up_preact):
    x, zh, c, zl, y = (lax.axis_index(a) for a in ("x", "zh", "c", "zl", "y"))
    states = (master_weight, first_moment, second_moment, gradient)
    own = adamw(*states)[0].astype(bf16)

    def by_core(low, high, axis, move):
        pairs = [(2 * i + k, 2 * move(i, k) + k) for i in range(4) for k in range(2)]
        return lax.ppermute(jnp.where(c == 0, low, high), (axis, "c"), pairs)

    def onward(b3, b1):
        return by_core(b3, b1, "x", lambda i, k: (i + 1 - 2 * k) % X)

    q = (((x & 1) << 1) | (zh >> 1)) ^ y
    q = jnp.full((1,), q, jnp.int32)

    x20 = shift(own, "x", 2)
    x10 = shift(own, "x", -1)
    x30 = shift(own, "x", 1)
    z1 = flip(own, "zh", 1)
    z3 = flip(own, "zh", 3)
    gate_preact, up_preact, own, *states = in_order(gate_preact, up_preact, own, *states)
    hidden = hidden_of(gate_preact.T, up_preact.T)
    news = adamw(*states)
    x20, x10, x30, z1, z3, hidden, *news = in_order(x20, x10, x30, z1, z3, hidden, *news)
    new_weight, new_first, new_second = news

    other = shift(hidden, "c", 1)
    z2 = by_core(z3, z1, "zh", lambda i, k: i ^ (1 if k == 0 else 3))
    x33 = shift(z3, "x", 1)
    x13 = shift(z3, "x", -1)
    x33, x13, z1, other = in_order(x33, x13, z1, other)

    def sent(parts):
        return [parts[0]] + [flip(parts[d], "y", d) for d in (2, 3, 1)]

    def summed(parts):
        total = parts[0].astype(f32)
        for part in parts[1:]:
            total = total + part.astype(f32)
        return total.astype(bf16)

    x23 = onward(x33, x13)
    x31 = shift(z1, "x", 1)
    x11 = shift(z1, "x", -1)
    near_a = sent(round_of(q, hidden, other, [own, z3, x30, x33]))
    x31, x11, z2 = in_order(x31, x11, z2)

    x32 = shift(z2, "x", 1)
    x12 = shift(z2, "x", -1)
    far_a = sent(round_of(q, hidden, other, [x20, x23, x10, x13]))
    x21 = onward(x31, x11)
    x32, x12, *near_a = in_order(x32, x12, *near_a)
    near_a = summed(near_a)

    x22 = onward(x32, x12)
    near_b = sent(round_of(q, hidden, other, [z1, z2, x31, x32]))
    x21, x22, *far_a = in_order(x21, x22, *far_a)
    far_a = summed(far_a)

    def finished(near, far):
        near_x = jnp.where((x & 1) == (y >> 1), x, (x + 3) & 3)
        keep_near = (near_x >> 1) == zl
        keep = jnp.where(keep_near, near, far)
        send = jnp.where(keep_near, far, near)
        value = (keep.astype(f32) + flip(send, "zl", 1).astype(f32)).astype(bf16)
        return value[:512], flip(value[512:], "c", 1)

    first = finished(near_a, far_a)
    far_b = summed(sent(round_of(q, hidden, other, [x21, x22, x11, x12])))
    near_b = summed(near_b)
    second = finished(near_b, far_b)

    first_half = (zh & 1) ^ (zh >> 1) ^ (y & 1)
    columns = []
    for a in range(2):
        for b in range(2):
            mine = jnp.where(first_half == a, first[0], second[0])
            theirs = jnp.where(first_half == a, first[1], second[1])
            columns.append(jnp.where(c == b, mine, theirs))
    return (new_weight, new_first, new_second, jnp.concatenate(columns, axis=1))


def solution(mesh):
    fine = Mesh(mesh.devices.reshape(X, ZH, C, ZL, Y), ("x", "zh", "c", "zl", "y"))
    wide, tp = ("x", "zh", "c"), ("zl", "y")
    in_specs = (P(tp, wide),) * 4 + (P(wide, tp),) * 2
    out_specs = (P(tp, wide),) * 3 + (P(wide, tp),)
    return jax.shard_map(body, mesh=fine, in_specs=in_specs, out_specs=out_specs, check_vma=False)
```
